32 devices in a mesh: doc: 4 (over z), gram: 8 (over y, x, core).
Axes of the slice: x: 2, y: 2, z: 4, core: 2. Of those that a mesh axis runs over, the one named last changes fastest.
Arguments:
- w_factor: bfloat16 [6144, 256], P(('doc', 'gram')), may hold values from 0.003 to 0.1
- h_factor: bfloat16 [12288, 256], P(('gram', 'doc')), may hold values from 0.003 to 0.1
- tile_counts: bfloat16 [4, 8, 24, 128, 128], P('doc', 'gram'), may hold values from 0 to 30, as said below
- tile_rows: int32 [4, 8, 24], P('doc', 'gram'), may hold values from 0 to 11, as said below
- tile_cols: int32 [4, 8, 24], P('doc', 'gram'), may hold values from 0 to 11, as said below
- tile_live: int32 [4, 8], P('doc', 'gram'), may hold values from 1 to 24, as said below
Outputs:
- w_next: bfloat16 [6144, 256], P(('doc', 'gram'))
- h_next: bfloat16 [12288, 256], P(('gram', 'doc'))
The draws below stay inside these ranges and needn't reach their ends.
Inputs may be any that keep to these rules, and one draw needn't show every extreme that they name: `tile_rows`: within one device pair the first tile_live slots name distinct tiles; slots hold positions in every case. `tile_cols`: see tile_rows. `tile_live`: some device pair holds 24 tiles. `tile_counts`: whole numbers.
All inputs are finite; a program needn't handle non-finite values.
Results may differ from the reference program's by a relative error of at most 0.0021.
Values may be sent and summed in bfloat16 or wider, within the bound.
No kernel may reach another device: no remote copies, remote signals or barrier semaphores. Data moves between devices by JAX's collectives and lax.ppermute only.
A program may use at most 64 MiB of HBM per device.

```python
import jax
import jax.numpy as jnp
from jax import lax

TOPICS = 256
TILE = 128
TR = 12
TC = 12
SLOTS = 24
DOCS = 6144
NGRAMS = 12288
N_DOC = 4
N_GRAM = 8


def draw_w_factor(key, part):
    place = jnp.arange(DOCS, dtype=jnp.float32)[:, None]
    rising = 1.0 + 2.0 * place / DOCS
    base = 0.01 * jnp.exp(jax.random.uniform(key, (DOCS, TOPICS), jnp.float32, -1.0, 1.0))
    return (base * rising).astype(jnp.bfloat16)


def draw_h_factor(key, part):
    place = jnp.arange(NGRAMS, dtype=jnp.float32)[:, None]
    rising = 1.0 + 2.0 * place / NGRAMS
    base = 0.01 * jnp.exp(jax.random.uniform(key, (NGRAMS, TOPICS), jnp.float32, -1.0, 1.0))
    return (base * rising).astype(jnp.bfloat16)


def draw_tile_counts(key, part):
    shape = (N_DOC, N_GRAM, SLOTS, TILE, TILE)
    first, second = jax.random.split(key)
    present = jax.random.randint(first, shape, 0, 5) < 2
    values = jax.random.randint(second, shape, 1, 16)
    return jnp.where(present, values, 0).astype(jnp.float32).astype(jnp.bfloat16)


def tile_places(key):
    base = jax.random.fold_in(key, 7)
    keys = jax.random.split(base, N_DOC * N_GRAM)
    orders = jax.vmap(lambda one: jax.random.permutation(one, TR * TC))(keys)[:, :SLOTS]
    return orders.reshape(N_DOC, N_GRAM, SLOTS).astype(jnp.int32)


def draw_tile_rows(key, part):
    return tile_places(key) // TC


def draw_tile_cols(key, part):
    return tile_places(key) % TC


def draw_tile_live(key, part):
    base = jax.random.fold_in(key, 11)
    lots = jax.random.randint(base, (N_DOC * N_GRAM,), SLOTS // 4, SLOTS + 1)
    chosen = jax.random.randint(jax.random.fold_in(base, 3), (), 0, N_DOC * N_GRAM)
    lots = jnp.where(jnp.arange(N_DOC * N_GRAM, dtype=jnp.int32) == chosen, SLOTS, lots)
    return lots.reshape(N_DOC, N_GRAM).astype(jnp.int32)


def setup_inputs(seed: int = 0) -> dict:
    streams_of = jax.random.split(jax.random.key(seed), 7)
    return {
        "w_factor": draw_w_factor(jax.random.fold_in(streams_of[6], 71), 0),
        "h_factor": draw_h_factor(jax.random.fold_in(streams_of[6], 71), 0),
        "tile_counts": draw_tile_counts(jax.random.fold_in(streams_of[6], 71), 0),
        "tile_rows": draw_tile_rows(jax.random.fold_in(streams_of[6], 71), 0),
        "tile_cols": draw_tile_cols(jax.random.fold_in(streams_of[6], 71), 0),
        "tile_live": draw_tile_live(jax.random.fold_in(streams_of[6], 71), 0),
    }


def pair_terms(w_tiles, h_tiles, rows, cols, counts, live):
    width = rows.shape[0]
    wt = jnp.take(w_tiles, rows, axis=0).astype(jnp.float32)
    ht = jnp.take(h_tiles, cols, axis=0).astype(jnp.float32)
    model = jnp.einsum('spk,sqk->spq', wt, ht)
    keep = (jnp.arange(width, dtype=jnp.int32) < live).astype(jnp.float32)
    ratio = (counts.astype(jnp.float32) / model * keep[:, None, None]).astype(jnp.bfloat16)
    ratio_f = ratio.astype(jnp.float32)
    w_part = jnp.einsum('spq,sqk->spk', ratio_f, ht)
    h_part = jnp.einsum('spq,spk->sqk', ratio_f, wt)
    pick_r = (rows[:, None] == jnp.arange(w_tiles.shape[0], dtype=jnp.int32)[None, :]).astype(jnp.float32)
    pick_c = (cols[:, None] == jnp.arange(h_tiles.shape[0], dtype=jnp.int32)[None, :]).astype(jnp.float32)
    add_w = jnp.einsum('st,spk->tpk', pick_r, w_part, precision=lax.Precision.HIGHEST)
    add_h = jnp.einsum('st,spk->tpk', pick_c, h_part, precision=lax.Precision.HIGHEST)
    return add_w, add_h


def reference(w_factor, h_factor, tile_counts, tile_rows, tile_cols, tile_live):
    w_blocks = w_factor.reshape(N_DOC, TR, TILE, TOPICS)
    h_blocks = h_factor.reshape(N_GRAM, TC, TILE, TOPICS)
    pairs = jnp.arange(N_DOC * N_GRAM, dtype=jnp.int32)

    def visit(carry, pair):
        w_numer, h_numer = carry
        d = pair // N_GRAM
        g = pair % N_GRAM
        add_w, add_h = pair_terms(w_blocks[d], h_blocks[g], tile_rows[d, g], tile_cols[d, g], tile_counts[d, g], tile_live[d, g])
        return (w_numer.at[d].add(add_w), h_numer.at[g].add(add_h)), None

    start = (jnp.zeros((N_DOC, TR, TILE, TOPICS), jnp.float32), jnp.zeros((N_GRAM, TC, TILE, TOPICS), jnp.float32))
    (w_numer, h_numer), _ = lax.scan(visit, start, pairs)
    w_denom = jnp.sum(h_factor.astype(jnp.float32), axis=0)
    h_denom = jnp.sum(w_factor.astype(jnp.float32), axis=0)
    w_next = (w_factor.astype(jnp.float32) * w_numer.reshape(DOCS, TOPICS) / w_denom).astype(jnp.bfloat16)
    h_next = (h_factor.astype(jnp.float32) * h_numer.reshape(NGRAMS, TOPICS) / h_denom).astype(jnp.bfloat16)
    return w_next, h_next
```

```python
import functools

import jax
import jax.numpy as jnp
from jax import lax
from jax.experimental import pallas as pl
from jax.experimental.pallas import tpu as pltpu
from jax.sharding import PartitionSpec as P

OUTER = 4
EXTRA = 8
UNROLL = 4
W_SCALE = 2.0**-6
H_SCALE = 2.0**-5
GROUPS = ((0, 2, 1), (3,))


def partner(axis, outer, inner, by_outer, by_inner):
    return [
        ((o * inner + i), (o ^ by_outer) * inner + (i ^ by_inner))
        for o in range(outer)
        for i in range(inner)
    ]


def split_sums(sums):
    high = sums.astype(jnp.bfloat16).astype(jnp.float32)
    place = lax.broadcasted_iota(jnp.int32, sums.shape, 0)
    return jnp.where(place == 0, high, jnp.where(place == 1, sums - high, 0.0))


def column_sums(block):
    return jnp.dot(
        jnp.ones((EXTRA, block.shape[0]), jnp.bfloat16), block, preferred_element_type=jnp.float32
    )


def tiles_kernel(plan, *refs):
    group, first, last, side, inner, w_rows = plan
    rows, cols, live, w_ref, counts = refs[:5]
    refs = refs[5:]
    width = len(group)
    h_pieces, refs = refs[:width], refs[width:]
    acc_in, refs = (None, refs) if first else (refs[0], refs[1:])
    h_outs, refs = refs[:width], refs[width:]
    out, refs = refs[0], refs[1:]
    order, h_all, h_sum, refs = refs[0], refs[1], refs[2], refs[3:]
    acc = refs[0] if last else out
    quarter = h_pieces[0].shape[0]
    me_h = lax.axis_index("doc") // (lax.axis_size("doc") // OUTER)
    w_len = w_ref.shape[0]

    count = live[0, 0]

    def scan(slot, found):
        near = (cols[0, 0, slot] * side) // quarter ^ me_h
        hit = near == group[0]
        for member in group[1:]:
            hit = hit | (near == member)
        order[found] = slot
        return found + jnp.where(hit, 1, 0)

    found = lax.fori_loop(0, count, scan, 0)
    for extra in range(UNROLL):
        order[found + extra] = 0

    sums = column_sums(h_pieces[0][...])
    for piece in h_pieces[1:]:
        sums = sums + column_sums(piece[...])
    if first:
        acc[...] = jnp.zeros_like(acc)
        acc[w_len:, :] = sums
    else:
        acc[:w_len, :] = acc_in[:w_len, :]
        acc[w_len:, :] = acc_in[w_len:, :] + sums
    for at, piece in enumerate(h_pieces):
        h_all[at * quarter : (at + 1) * quarter, :] = piece[...]
    h_sum[...] = jnp.zeros_like(h_sum)

    def place_of(slot):
        col = cols[0, 0, slot] * side
        near = col // quarter ^ me_h
        local = lax.rem(col, quarter)
        at = jnp.int32(0)
        for k, member in enumerate(group):
            at = jnp.where(near == member, k, at)
        return pl.multiple_of(at * quarter + local, side)

    def visit(step, carry):
        terms = []
        for k in range(UNROLL):
            j = step * UNROLL + k
            slot = order[j]
            row = pl.multiple_of(rows[0, 0, slot] * side, side)
            col = place_of(slot)
            wt = w_ref[pl.ds(row, side), :]
            ht = h_all[pl.ds(col, side), :]
            model = lax.dot_general(
                wt, ht, (((1,), (1,)), ((), ())), preferred_element_type=jnp.float32
            )
            keep = jnp.where(j < found, 1.0, 0.0)
            ratio = (counts[0, 0, slot].astype(jnp.float32) / model * keep).astype(jnp.bfloat16)
            w_part = jnp.dot(ratio, ht, preferred_element_type=jnp.float32)
            h_part = lax.dot_general(
                ratio, wt, (((0,), (0,)), ((), ())), preferred_element_type=jnp.float32
            )
            terms.append((row, col, w_part, h_part))
        for row, col, w_part, h_part in terms:
            acc[pl.ds(row, side), :] += w_part
            h_sum[pl.ds(col, side), :] += h_part
        return carry

    lax.fori_loop(0, (found + UNROLL - 1) // UNROLL, visit, 0)

    w_sums = split_sums(column_sums(w_ref[...]))
    for at, h_out in enumerate(h_outs):
        h_out[:quarter, :] = h_sum[at * quarter : (at + 1) * quarter, :]
        h_out[quarter:, :] = w_sums
    if last:
        me_w = lax.axis_index("gram")
        me_o, me_i = me_w // inner, lax.rem(me_w, inner)
        tail = split_sums(acc[w_len:, :])
        for i in range(inner):
            for o in range(OUTER):
                piece = (me_o ^ o) * inner + (me_i ^ i)
                at = pl.multiple_of(piece * w_rows, 8)
                out[i, o, :w_rows, :] = acc[pl.ds(at, w_rows), :]
                out[i, o, w_rows:, :] = tail


def tiles_call(group, first, last, places, w_block, counts, h_pieces, acc, inner, w_rows):
    side = counts.shape[-1]
    slots = counts.shape[2]
    topics = w_block.shape[1]
    quarter = h_pieces[0].shape[0]
    width = len(group)
    plan = (group, first, last, side, inner, w_rows)
    smem = pl.BlockSpec(memory_space=pltpu.SMEM)
    vmem = pl.BlockSpec(memory_space=pltpu.VMEM)
    acc_shape = (w_block.shape[0] + EXTRA, topics)
    out_shape = (inner, OUTER, w_rows + EXTRA, topics) if last else acc_shape
    scratch = [
        pltpu.SMEM((slots + UNROLL,), jnp.int32),
        pltpu.VMEM((width * quarter, topics), jnp.bfloat16),
        pltpu.VMEM((width * quarter, topics), jnp.float32),
    ]
    if last:
        scratch.append(pltpu.VMEM(acc_shape, jnp.float32))
    args = [*places, w_block, counts, *h_pieces] + ([] if first else [acc])
    outs = pl.pallas_call(
        functools.partial(tiles_kernel, plan),
        out_shape=[
            *[jax.ShapeDtypeStruct((quarter + EXTRA, topics), jnp.float32)] * width,
            jax.ShapeDtypeStruct(out_shape, jnp.float32),
        ],
        in_specs=[smem] * 3 + [vmem] * (len(args) - 3),
        out_specs=[vmem] * (width + 1),
        scratch_shapes=scratch,
        compiler_params=pltpu.CompilerParams(vmem_limit_bytes=40 * 1024 * 1024),
        cost_estimate=pl.CostEstimate(
            flops=6 * 6 * width * side * side * topics, bytes_accessed=1 << 22, transcendentals=0
        ),
    )(*args)
    return outs[:width], outs[width]


def body(w_factor, h_factor, tile_counts, tile_rows, tile_cols, tile_live):
    doc, gram = lax.axis_size("doc"), lax.axis_size("gram")
    inner_h, inner_w = doc // OUTER, gram // OUTER
    w_rows, topics = w_factor.shape
    h_rows = h_factor.shape[0]

    def send_h(x, by_outer, by_inner):
        return lax.ppermute(x, "doc", partner("doc", OUTER, inner_h, by_outer, by_inner))

    def send_w(x, by_outer, by_inner):
        return lax.ppermute(x, "gram", partner("gram", OUTER, inner_w, by_outer, by_inner))

    if inner_h > 1:
        ring = [[o * inner_h + i for i in range(inner_h)] for o in range(OUTER)]
        mine = lax.all_gather(h_factor, "doc", axis=0, tiled=True, axis_index_groups=ring)
    else:
        mine = h_factor
    pieces = {0: mine, 2: send_h(mine, 2, 0), 1: send_h(mine, 1, 0), 3: send_h(mine, 3, 0)}
    w_block = lax.all_gather(w_factor, "gram", axis=0, tiled=True)

    places = (tile_rows, tile_cols, tile_live)
    acc = None
    h_terms = {}
    for at, group in enumerate(GROUPS):
        parts, acc = tiles_call(
            group,
            at == 0,
            at == len(GROUPS) - 1,
            places,
            w_block,
            tile_counts,
            [pieces[m] for m in group],
            acc,
            inner_w,
            w_rows,
        )
        for m, part in zip(group, parts):
            h_terms[m] = part if m == 0 else send_h((part * H_SCALE).astype(jnp.float16), m, 0)

    w_terms = acc[0]
    for i in range(1, inner_w):
        w_terms = w_terms + send_w(acc[i], 0, i)
    w_total = w_terms[0] * W_SCALE
    for o in range(1, OUTER):
        w_total = w_total + send_w((w_terms[o] * W_SCALE).astype(jnp.float16), o, 0).astype(
            jnp.float32
        )
    w_denom = jnp.sum(w_total[w_rows:], axis=0)
    w_next = (w_factor.astype(jnp.float32) * w_total[:w_rows] / w_denom).astype(jnp.bfloat16)

    h_total = h_terms[0] * H_SCALE
    for m in range(1, OUTER):
        h_total = h_total + h_terms[m].astype(jnp.float32)
    if inner_h > 1:
        me_i = lax.rem(lax.axis_index("doc"), inner_h)
        tail = h_total[-EXTRA:]

        def share(i):
            part = lax.dynamic_slice_in_dim(h_total, (me_i ^ i) * h_rows, h_rows, 0)
            return jnp.concatenate([part, tail], axis=0)

        total = share(0)
        for i in range(1, inner_h):
            total = total + send_h(share(i), 0, i)
        h_total = total
    h_denom = jnp.sum(h_total[h_rows:], axis=0)
    h_next = (h_factor.astype(jnp.float32) * h_total[:h_rows] / h_denom).astype(jnp.bfloat16)
    return (w_next, h_next)


def solution(mesh):
    in_specs = (
        P(("doc", "gram"), None),
        P(("gram", "doc"), None),
        P("doc", "gram", None, None, None),
        P("doc", "gram", None),
        P("doc", "gram", None),
        P("doc", "gram"),
    )
    out_specs = (P(("doc", "gram"), None), P(("gram", "doc"), None))
    return jax.shard_map(body, mesh=mesh, in_specs=in_specs, out_specs=out_specs, check_vma=False)
```

```python
import functools

import jax
import jax.numpy as jnp
from jax import lax
from jax.experimental import pallas as pl
from jax.experimental.pallas import tpu as pltpu
from jax.sharding import PartitionSpec as P

OUTER = 4
EXTRA = 8
STEP_RATIO = 8
STEP_SUM = 4
SCALE = 2.0**-5
FIRST_GROUP = (3,)
LAST_GROUP = (0, 1, 2)


def partner(outer, inner, by_outer, by_inner):
    return [
        ((o * inner + i), (o ^ by_outer) * inner + (i ^ by_inner))
        for o in range(outer)
        for i in range(inner)
    ]


def partial_sums(block):
    rows, k = block.shape
    return jnp.sum(block.astype(jnp.float32).reshape(rows // EXTRA, EXTRA, k), axis=0)


def visit_tiles(
    group, side, w_ref, counts, acc, h_outs, order, ratios, h_all, h_sum, rows, cols, live
):
    quarter = h_all.shape[0] // len(group)
    me_h = lax.axis_index("doc") // (lax.axis_size("doc") // OUTER)

    def quarter_of(slot):
        return (cols[0, 0, slot] * side) // quarter ^ me_h

    def scan(slot, found):
        near = quarter_of(slot)
        hit = near == group[0]
        for member in group[1:]:
            hit = hit | (near == member)
        order[found] = slot
        return found + jnp.where(hit, 1, 0)

    found = lax.fori_loop(0, live[0, 0], scan, 0)
    for extra in range(max(STEP_RATIO, STEP_SUM)):
        order[found + extra] = 0

    def tile_at(j):
        slot = order[j]
        near = quarter_of(slot)
        at = jnp.int32(0)
        for k, member in enumerate(group):
            at = jnp.where(near == member, k, at)
        row = pl.multiple_of(rows[0, 0, slot] * side, side)
        col = at * quarter + lax.rem(cols[0, 0, slot] * side, quarter)
        return slot, row, pl.multiple_of(col, side)

    def make_ratios(step, carry):
        made = []
        for k in range(STEP_RATIO):
            j = step * STEP_RATIO + k
            slot, row, col = tile_at(j)
            model = lax.dot_general(
                w_ref[pl.ds(row, side), :],
                h_all[pl.ds(col, side), :],
                (((1,), (1,)), ((), ())),
                preferred_element_type=jnp.float32,
            )
            keep = jnp.where(j < found, 1.0, 0.0)
            made.append((counts[slot].astype(jnp.float32) / model * keep).astype(jnp.bfloat16))
        for k, ratio in enumerate(made):
            ratios[step * STEP_RATIO + k] = ratio
        return carry

    def add_terms(step, carry):
        terms = []
        for k in range(STEP_SUM):
            j = step * STEP_SUM + k
            slot, row, col = tile_at(j)
            ratio = ratios[j]
            w_part = jnp.dot(
                ratio, h_all[pl.ds(col, side), :], preferred_element_type=jnp.float32
            )
            h_part = lax.dot_general(
                ratio,
                w_ref[pl.ds(row, side), :],
                (((0,), (0,)), ((), ())),
                preferred_element_type=jnp.float32,
            )
            terms.append((row, col, w_part, h_part))
        for row, col, w_part, h_part in terms:
            acc[pl.ds(row, side), :] += w_part
            h_sum[pl.ds(col, side), :] += h_part
        return carry

    lax.fori_loop(0, (found + STEP_RATIO - 1) // STEP_RATIO, make_ratios, 0)
    lax.fori_loop(0, (found + STEP_SUM - 1) // STEP_SUM, add_terms, 0)

    w_sums = partial_sums(w_ref[...])
    for at, h_out in enumerate(h_outs):
        h_out[:quarter, :] = h_sum[at * quarter : (at + 1) * quarter, :]
        h_out[quarter:, :] = w_sums


def started(sems, *pairs):
    copies = [
        pltpu.make_async_copy(source, target, sems.at[k])
        for k, (source, target) in enumerate(pairs)
    ]
    for copy in copies:
        copy.start()
    return copies


def first_kernel(group, side, inner, rows_in, cols_in, live, stored, w_block, *refs):
    h_pieces, refs = refs[: len(group)], refs[len(group) :]
    acc, counts, refs = refs[0], refs[1], refs[2:]
    h_outs, refs = refs[: len(group)], refs[len(group) :]
    sems, order, ratios, h_all, h_sum, rows, cols = refs
    copies = started(sems, (rows_in, rows), (cols_in, cols), (stored.at[0, 0], counts))
    quarter = h_pieces[0].shape[0]
    w_len = w_block.shape[0]
    for at, piece in enumerate(h_pieces):
        h_all[at * quarter : (at + 1) * quarter, :] = piece[...]
    acc[:w_len, :] = jnp.zeros((w_len, acc.shape[1]), jnp.float32)
    acc[w_len:, :] = partial_sums(h_all[...])
    h_sum[...] = jnp.zeros_like(h_sum)
    for copy in copies:
        copy.wait()
    visit_tiles(
        group, side, w_block, counts, acc, h_outs, order, ratios, h_all, h_sum, rows, cols, live
    )


def last_kernel(group, side, inner, rows_in, cols_in, live, counts, w_block, acc_in, *refs):
    mine, h_pieces, refs = refs[0], refs[1 : len(group)], refs[len(group) :]
    w_outs, refs = refs[:inner], refs[inner:]
    h_outs, refs = refs[: len(group)], refs[len(group) :]
    sems, order, ratios, h_all, h_sum, rows, cols, acc = refs
    quarter = mine.shape[0]
    copies = started(
        sems, (rows_in, rows), (cols_in, cols), (mine, h_all.at[pl.ds(0, quarter)])
    )
    w_len = w_block.shape[0]
    w_rows = w_len // (inner * OUTER)
    for at, piece in enumerate(h_pieces):
        h_all[(at + 1) * quarter : (at + 2) * quarter, :] = piece[...]
    acc[:w_len, :] = acc_in[:w_len, :]
    h_sum[...] = jnp.zeros_like(h_sum)
    for copy in copies:
        copy.wait()
    acc[w_len:, :] = acc_in[w_len:, :] + partial_sums(h_all[...])
    visit_tiles(
        group, side, w_block, counts, acc, h_outs, order, ratios, h_all, h_sum, rows, cols, live
    )
    me_w = lax.axis_index("gram")
    me_o, me_i = me_w // inner, lax.rem(me_w, inner)
    for i in range(inner):
        for o in range(OUTER):
            at = pl.multiple_of(((me_o ^ o) * inner + (me_i ^ i)) * w_rows, 8)
            w_outs[i][o, :w_rows, :] = acc[pl.ds(at, w_rows), :]
            w_outs[i][o, w_rows:, :] = acc[w_len:, :]


def in_hbm(x):
    return pltpu.with_memory_space_constraint(x, pltpu.HBM)


def run_kernel(kernel, group, inner, args, from_hbm, out_shapes, quarter, acc_shape):
    rows, cols, _, counts = args[:4]
    slots, side = counts.shape[-3:-1]
    topics = acc_shape[1]
    width = len(group)
    pad = max(STEP_RATIO, STEP_SUM)
    scratch = [
        pltpu.SemaphoreType.DMA((3,)),
        pltpu.SMEM((slots + pad,), jnp.int32),
        pltpu.VMEM((slots + pad, side, side), jnp.bfloat16),
        pltpu.VMEM((width * quarter, topics), jnp.bfloat16),
        pltpu.VMEM((width * quarter, topics), jnp.float32),
        pltpu.SMEM(rows.shape, rows.dtype),
        pltpu.SMEM(cols.shape, cols.dtype),
    ]
    if kernel is last_kernel:
        scratch.append(pltpu.VMEM(acc_shape, jnp.float32))
    spaces = [pltpu.HBM if at in from_hbm else pltpu.VMEM for at in range(len(args))]
    spaces[2] = pltpu.SMEM
    args = [in_hbm(x) if at in from_hbm else x for at, x in enumerate(args)]
    return pl.pallas_call(
        functools.partial(kernel, group, side, inner),
        out_shape=out_shapes,
        in_specs=[pl.BlockSpec(memory_space=space) for space in spaces],
        out_specs=[pl.BlockSpec(memory_space=pltpu.VMEM)] * len(out_shapes),
        scratch_shapes=scratch,
        compiler_params=pltpu.CompilerParams(vmem_limit_bytes=32 * 1024 * 1024),
        cost_estimate=pl.CostEstimate(
            flops=36 * width * side * side * topics, bytes_accessed=1 << 23, transcendentals=0
        ),
    )(*args)


def body(w_factor, h_factor, tile_counts, tile_rows, tile_cols, tile_live):
    doc, gram = lax.axis_size("doc"), lax.axis_size("gram")
    inner_h, inner_w = doc // OUTER, gram // OUTER
    w_rows, topics = w_factor.shape
    h_rows = h_factor.shape[0]
    w_len = w_rows * gram

    def send_h(x, by_outer, by_inner=0):
        return lax.ppermute(x, "doc", partner(OUTER, inner_h, by_outer, by_inner))

    def send_w(x, by_outer, by_inner=0):
        return lax.ppermute(x, "gram", partner(OUTER, inner_w, by_outer, by_inner))

    if inner_h > 1:
        ring = [[o * inner_h + i for i in range(inner_h)] for o in range(OUTER)]
        mine = lax.all_gather(h_factor, "doc", axis=0, tiled=True, axis_index_groups=ring)
    else:
        mine = h_factor
    quarter = mine.shape[0]
    h_pieces = {0: mine}
    for m in (3, 2, 1):
        h_pieces[m] = send_h(mine, m)
    w_block = lax.all_gather(w_factor, "gram", axis=0, tiled=True)

    places = [tile_rows, tile_cols, tile_live]
    acc_shape = jax.ShapeDtypeStruct((w_len + EXTRA, topics), jnp.float32)
    h_shape = jax.ShapeDtypeStruct((quarter + EXTRA, topics), jnp.float32)
    w_shape = jax.ShapeDtypeStruct((OUTER, w_rows + EXTRA, topics), jnp.float32)
    acc, counts, far = run_kernel(
        first_kernel,
        FIRST_GROUP,
        inner_w,
        [*places, tile_counts, w_block, *[h_pieces[m] for m in FIRST_GROUP]],
        (0, 1, 3),
        [acc_shape, jax.ShapeDtypeStruct(tile_counts.shape[2:], tile_counts.dtype), h_shape],
        quarter,
        acc_shape.shape,
    )
    h_scale = SCALE / 2
    far = send_h((far * h_scale).astype(jnp.float16), 1)
    outs = run_kernel(
        last_kernel,
        LAST_GROUP,
        inner_w,
        [*places, counts, w_block, acc, *[h_pieces[m] for m in LAST_GROUP]],
        (0, 1, 6),
        [w_shape] * inner_w + [h_shape] * len(LAST_GROUP),
        quarter,
        acc_shape.shape,
    )
    far, *w_outs = lax.optimization_barrier((far, *outs[:inner_w]))
    terms = dict(zip(LAST_GROUP, outs[inner_w:]))
    across = (terms[2] * h_scale + far.astype(jnp.float32)).astype(jnp.float16)
    across = send_h(across, 2)

    w_scale = SCALE / inner_w
    w_got = [send_w(w_outs[i], 0, i) for i in range(1, inner_w)]
    near, *w_got = lax.optimization_barrier(((terms[1] * h_scale).astype(jnp.float16), *w_got))
    near = send_h(near, 1)
    w_terms = w_outs[0]
    for got in w_got:
        w_terms = w_terms + got
    w_sent = [
        send_w((w_terms[o] * w_scale).astype(jnp.float16), o) for o in range(1, OUTER)
    ]

    h_total = terms[0] * h_scale + across.astype(jnp.float32) + near.astype(jnp.float32)
    if inner_h > 1:
        me_i = lax.rem(lax.axis_index("doc"), inner_h)
        tail = h_total[-EXTRA:]

        def share(i):
            part = lax.dynamic_slice_in_dim(h_total, (me_i ^ i) * h_rows, h_rows, 0)
            return jnp.concatenate([part, tail], axis=0)

        total = share(0)
        for i in range(1, inner_h):
            total = total + send_h(share(i), 0, i)
        h_total = total
    h_denom = jnp.sum(h_total[h_rows:], axis=0)
    h_next = (h_factor.astype(jnp.float32) * h_total[:h_rows] / h_denom).astype(jnp.bfloat16)

    h_next, *w_sent = lax.optimization_barrier((h_next, *w_sent))
    w_total = w_terms[0] * w_scale
    for got in w_sent:
        w_total = w_total + got.astype(jnp.float32)
    w_denom = jnp.sum(w_total[w_rows:], axis=0)
    w_next = (w_factor.astype(jnp.float32) * w_total[:w_rows] / w_denom).astype(jnp.bfloat16)
    return (w_next, h_next)


def solution(mesh):
    in_specs = (
        P(("doc", "gram"), None),
        P(("gram", "doc"), None),
        P("doc", "gram", None, None, None),
        P("doc", "gram", None),
        P("doc", "gram", None),
        P("doc", "gram"),
    )
    out_specs = (P(("doc", "gram"), None), P(("gram", "doc"), None))
    return jax.shard_map(body, mesh=mesh, in_specs=in_specs, out_specs=out_specs, check_vma=False)
```

```python
import functools

import jax
import jax.numpy as jnp
from jax import lax
from jax.experimental import pallas as pl
from jax.experimental.pallas import tpu as pltpu
from jax.sharding import PartitionSpec as P

OUTER = 4
EXTRA = 8
STEP_RATIO = 8
STEP_SUM = 4
SCALE = 2.0**-5
FIRST_GROUP = (3,)
MIDDLE_GROUP = (0, 1)
LAST_GROUP = (2,)


def partner(outer, inner, by_outer, by_inner):
    return [
        ((o * inner + i), (o ^ by_outer) * inner + (i ^ by_inner))
        for o in range(outer)
        for i in range(inner)
    ]


def partial_sums(block):
    rows, k = block.shape
    return jnp.sum(block.astype(jnp.float32).reshape(rows // EXTRA, EXTRA, k), axis=0)


def visit_tiles(group, side, w_ref, counts, ready, acc, h_out, order, ratios, h_all, rows, cols, live):
    quarter = h_all.shape[0] // len(group)
    me_h = lax.axis_index("doc") // (lax.axis_size("doc") // OUTER)

    def quarter_of(slot):
        return (cols[0, 0, slot] * side) // quarter ^ me_h

    def scan(slot, found):
        near = quarter_of(slot)
        hit = near == group[0]
        for member in group[1:]:
            hit = hit | (near == member)
        order[found] = slot
        return found + jnp.where(hit, 1, 0)

    found = lax.fori_loop(0, live[0, 0], scan, 0)
    for extra in range(max(STEP_RATIO, STEP_SUM)):
        order[found + extra] = 0

    def tile_at(j):
        slot = order[j]
        near = quarter_of(slot)
        at = jnp.int32(0)
        for k, member in enumerate(group):
            at = jnp.where(near == member, k, at)
        row = pl.multiple_of(rows[0, 0, slot] * side, side)
        local = pl.multiple_of(lax.rem(cols[0, 0, slot] * side, quarter), side)
        return slot, row, at, local, pl.multiple_of(at * quarter + local, side)

    def make_ratios(step, carry):
        made = []
        for k in range(STEP_RATIO):
            j = step * STEP_RATIO + k
            slot, row, _, _, col = tile_at(j)
            model = lax.dot_general(
                w_ref[pl.ds(row, side), :],
                h_all[pl.ds(col, side), :],
                (((1,), (1,)), ((), ())),
                preferred_element_type=jnp.float32,
            )
            keep = jnp.where(j < found, 1.0, 0.0)
            made.append((counts[slot].astype(jnp.float32) / model * keep).astype(jnp.bfloat16))
        for k, ratio in enumerate(made):
            ratios[step * STEP_RATIO + k] = ratio
        return carry

    def add_terms(step, carry):
        terms = []
        for k in range(STEP_SUM):
            j = step * STEP_SUM + k
            slot, row, at, local, col = tile_at(j)
            ratio = ratios[j]
            w_part = jnp.dot(
                ratio, h_all[pl.ds(col, side), :], preferred_element_type=jnp.float32
            )
            h_part = lax.dot_general(
                ratio,
                w_ref[pl.ds(row, side), :],
                (((0,), (0,)), ((), ())),
                preferred_element_type=jnp.float32,
            )
            terms.append((row, at, local, w_part, h_part))
        for row, at, local, w_part, h_part in terms:
            acc[pl.ds(row, side), :] += w_part
            h_out[at, pl.ds(local, side), :] += h_part
        return carry

    if ready is not None:
        ready()
    lax.fori_loop(0, (found + STEP_RATIO - 1) // STEP_RATIO, make_ratios, 0)
    lax.fori_loop(0, (found + STEP_SUM - 1) // STEP_SUM, add_terms, 0)


def clear(h_out, quarter, w_sums):
    for at in range(h_out.shape[0]):
        h_out[at, :quarter, :] = jnp.zeros((quarter, h_out.shape[2]), jnp.float32)
        h_out[at, quarter:, :] = w_sums


def started(sems, first, *pairs):
    copies = [
        pltpu.make_async_copy(source, target, sems.at[first + k])
        for k, (source, target) in enumerate(pairs)
    ]
    for copy in copies:
        copy.start()
    return copies


def first_kernel(group, side, inner, rows_in, cols_in, live, stored, w_pieces, *refs):
    h_pieces, refs = refs[: len(group)], refs[len(group) :]
    w_block, acc, counts, w_sums, h_out, sems, order, ratios, h_all, rows, cols = refs
    places = started(sems, 0, (rows_in, rows), (cols_in, cols))
    (load,) = started(sems, 2, (stored.at[0, 0], counts))
    quarter = h_pieces[0].shape[0]
    w_len = w_block.shape[0]
    w_rows = w_len // (inner * OUTER)
    me_o = lax.axis_index("gram") // inner
    for o in range(OUTER):
        for i in range(inner):
            at = pl.multiple_of(((me_o ^ o) * inner + i) * w_rows, 16)
            w_block[pl.ds(at, w_rows), :] = w_pieces[i, o]
    for at, piece in enumerate(h_pieces):
        h_all[at * quarter : (at + 1) * quarter, :] = piece[...]
    acc[:w_len, :] = jnp.zeros((w_len, acc.shape[1]), jnp.float32)
    acc[w_len:, :] = partial_sums(h_all[...])
    w_sums[...] = partial_sums(w_block[...])
    clear(h_out, quarter, w_sums[...])
    for copy in places:
        copy.wait()
    visit_tiles(
        group, side, w_block, counts, load.wait, acc, h_out, order, ratios, h_all, rows, cols, live
    )


def middle_kernel(group, side, inner, rows_in, cols_in, live, counts, w_block, _, w_sums, *refs):
    mine, h_pieces, refs = refs[0], refs[1 : len(group)], refs[len(group) :]
    acc, h_out, sems, order, ratios, h_all, rows, cols = refs
    quarter = mine.shape[0]
    places = started(sems, 0, (rows_in, rows), (cols_in, cols))
    (load,) = started(sems, 2, (mine, h_all.at[pl.ds(0, quarter)]))
    w_len = w_block.shape[0]
    for at, piece in enumerate(h_pieces):
        h_all[(at + 1) * quarter : (at + 2) * quarter, :] = piece[...]
    clear(h_out, quarter, w_sums[...])
    for copy in places:
        copy.wait()
    visit_tiles(
        group, side, w_block, counts, load.wait, acc, h_out, order, ratios, h_all, rows, cols, live
    )
    acc[w_len:, :] += partial_sums(h_all[...])


def last_kernel(group, side, inner, rows_in, cols_in, live, counts, w_block, _, w_sums, *refs):
    h_pieces, refs = refs[: len(group)], refs[len(group) :]
    acc, h_out, w_outs, refs = refs[0], refs[1], refs[2 : 2 + inner], refs[2 + inner :]
    sems, order, ratios, h_all, rows, cols = refs
    quarter = h_pieces[0].shape[0]
    places = started(sems, 0, (rows_in, rows), (cols_in, cols))
    w_len = w_block.shape[0]
    w_rows = w_len // (inner * OUTER)
    for at, piece in enumerate(h_pieces):
        h_all[at * quarter : (at + 1) * quarter, :] = piece[...]
    acc[w_len:, :] += partial_sums(h_all[...])
    clear(h_out, quarter, w_sums[...])
    for copy in places:
        copy.wait()
    visit_tiles(
        group, side, w_block, counts, None, acc, h_out, order, ratios, h_all, rows, cols, live
    )
    me_w = lax.axis_index("gram")
    me_o, me_i = me_w // inner, lax.rem(me_w, inner)
    for i in range(inner):
        for o in range(OUTER):
            at = pl.multiple_of(((me_o ^ o) * inner + (me_i ^ i)) * w_rows, 8)
            w_outs[i][o, :w_rows, :] = acc[pl.ds(at, w_rows), :]
            w_outs[i][o, w_rows:, :] = acc[w_len:, :]


def finish_kernel(w_factor, h_factor, w_total, h_total, w_next, h_next):
    for factor, total, out in ((h_factor, h_total, h_next), (w_factor, w_total, w_next)):
        rows = factor.shape[0]
        denom = jnp.sum(total[rows:, :], axis=0, keepdims=True)
        out[...] = (factor[...].astype(jnp.float32) * total[:rows, :] / denom).astype(out.dtype)


def finish(w_factor, h_factor, w_total, h_total):
    vmem = pl.BlockSpec(memory_space=pltpu.VMEM)
    return pl.pallas_call(
        finish_kernel,
        out_shape=[jax.ShapeDtypeStruct(x.shape, x.dtype) for x in (w_factor, h_factor)],
        in_specs=[vmem] * 4,
        out_specs=[vmem] * 2,
        compiler_params=pltpu.CompilerParams(vmem_limit_bytes=16 * 1024 * 1024),
    )(w_factor, h_factor, w_total, h_total)


def in_hbm(x):
    return pltpu.with_memory_space_constraint(x, pltpu.HBM)


def run_kernel(kernel, group, inner, args, from_hbm, out_shapes, quarter, acc_shape):
    rows, cols, _, counts = args[:4]
    slots, side = counts.shape[-3:-1]
    topics = acc_shape[1]
    width = len(group)
    pad = max(STEP_RATIO, STEP_SUM)
    scratch = [
        pltpu.SemaphoreType.DMA((3,)),
        pltpu.SMEM((slots + pad,), jnp.int32),
        pltpu.VMEM((slots + pad, side, side), jnp.bfloat16),
        pltpu.VMEM((width * quarter, topics), jnp.bfloat16),
        pltpu.SMEM(rows.shape, rows.dtype),
        pltpu.SMEM(cols.shape, cols.dtype),
    ]
    spaces = [pltpu.HBM if at in from_hbm else pltpu.VMEM for at in range(len(args))]
    spaces[2] = pltpu.SMEM
    args = [in_hbm(x) if at in from_hbm else x for at, x in enumerate(args)]
    return pl.pallas_call(
        functools.partial(kernel, group, side, inner),
        out_shape=out_shapes,
        in_specs=[pl.BlockSpec(memory_space=space) for space in spaces],
        out_specs=[pl.BlockSpec(memory_space=pltpu.VMEM)] * len(out_shapes),
        scratch_shapes=scratch,
        input_output_aliases={} if kernel is first_kernel else {5: 0},
        compiler_params=pltpu.CompilerParams(vmem_limit_bytes=32 * 1024 * 1024),
        cost_estimate=pl.CostEstimate(
            flops=36 * width * side * side * topics, bytes_accessed=1 << 23, transcendentals=0
        ),
    )(*args)


def body(w_factor, h_factor, tile_counts, tile_rows, tile_cols, tile_live):
    doc, gram = lax.axis_size("doc"), lax.axis_size("gram")
    inner_h, inner_w = doc // OUTER, gram // OUTER
    w_rows, topics = w_factor.shape
    h_rows = h_factor.shape[0]
    w_len = w_rows * gram

    def send_h(x, by_outer, by_inner=0):
        return lax.ppermute(x, "doc", partner(OUTER, inner_h, by_outer, by_inner))

    def send_w(x, by_outer, by_inner=0):
        return lax.ppermute(x, "gram", partner(OUTER, inner_w, by_outer, by_inner))

    if inner_h > 1:
        ring = [[o * inner_h + i for i in range(inner_h)] for o in range(OUTER)]
        mine = lax.all_gather(h_factor, "doc", axis=0, tiled=True, axis_index_groups=ring)
    else:
        mine = h_factor
    quarter = mine.shape[0]
    h_pieces = {0: mine}
    h_pieces[3] = send_h(mine, 3)
    w_got = [send_w(w_factor, o) for o in range(1, OUTER)]
    h_pieces[2] = send_h(h_pieces[3], 1)
    later, w_got[0] = lax.optimization_barrier((mine, w_got[0]))
    h_pieces[1] = send_h(later, 1)
    w_outer = jnp.stack([w_factor] + w_got)
    pairs = [[o * inner_w + i for i in range(inner_w)] for o in range(OUTER)]
    w_pieces = lax.all_gather(w_outer, "gram", axis_index_groups=pairs)

    places = [tile_rows, tile_cols, tile_live]
    acc_shape = jax.ShapeDtypeStruct((w_len + EXTRA, topics), jnp.float32)
    h_shape = [
        jax.ShapeDtypeStruct((len(group), quarter + EXTRA, topics), jnp.float32)
        for group in (FIRST_GROUP, MIDDLE_GROUP, LAST_GROUP)
    ]
    sum_shape = jax.ShapeDtypeStruct((EXTRA, topics), jnp.float32)
    w_shape = jax.ShapeDtypeStruct((OUTER, w_rows + EXTRA, topics), jnp.float32)
    w_block, acc, counts, w_sums, far = run_kernel(
        first_kernel,
        FIRST_GROUP,
        inner_w,
        [*places, tile_counts, w_pieces, *[h_pieces[m] for m in FIRST_GROUP]],
        (0, 1, 3),
        [
            jax.ShapeDtypeStruct((w_len, topics), w_factor.dtype),
            acc_shape,
            jax.ShapeDtypeStruct(tile_counts.shape[2:], tile_counts.dtype),
            sum_shape,
            h_shape[0],
        ],
        quarter,
        acc_shape.shape,
    )
    h_scale = SCALE / 2
    far = send_h((far[0] * h_scale).astype(jnp.float16), 1)
    acc, middle = run_kernel(
        middle_kernel,
        MIDDLE_GROUP,
        inner_w,
        [*places, counts, w_block, acc, w_sums, *[h_pieces[m] for m in MIDDLE_GROUP]],
        (0, 1, 7),
        [acc_shape, h_shape[1]],
        quarter,
        acc_shape.shape,
    )
    _, last, *w_outs = run_kernel(
        last_kernel,
        LAST_GROUP,
        inner_w,
        [*places, counts, w_block, acc, w_sums, *[h_pieces[m] for m in LAST_GROUP]],
        (0, 1),
        [acc_shape, h_shape[2]] + [w_shape] * inner_w,
        quarter,
        acc_shape.shape,
    )
    terms = {0: middle[0], 1: middle[1], 2: last[0]}
    far, *w_outs = lax.optimization_barrier((far, *w_outs))
    across = (terms[2] * h_scale + far.astype(jnp.float32)).astype(jnp.float16)
    across = send_h(across, 2)

    w_scale = SCALE / inner_w
    w_got = [send_w(w_outs[i], 0, i) for i in range(1, inner_w)]
    near, *w_got = lax.optimization_barrier(((terms[1] * h_scale).astype(jnp.float16), *w_got))
    near = send_h(near, 1)
    w_terms = w_outs[0]
    for got in w_got:
        w_terms = w_terms + got
    w_sent = [
        send_w((w_terms[o] * w_scale).astype(jnp.float16), o) for o in range(1, OUTER)
    ]

    h_total = terms[0] * h_scale + across.astype(jnp.float32) + near.astype(jnp.float32)
    if inner_h > 1:
        me_i = lax.rem(lax.axis_index("doc"), inner_h)
        tail = h_total[-EXTRA:]

        def share(i):
            part = lax.dynamic_slice_in_dim(h_total, (me_i ^ i) * h_rows, h_rows, 0)
            return jnp.concatenate([part, tail], axis=0)

        total = share(0)
        for i in range(1, inner_h):
            total = total + send_h(share(i), 0, i)
        h_total = total
    h_total, *w_sent = lax.optimization_barrier((h_total, *w_sent))
    w_total = w_terms[0] * w_scale
    for got in w_sent:
        w_total = w_total + got.astype(jnp.float32)
    w_next, h_next = finish(w_factor, h_factor, w_total, h_total)
    return (w_next, h_next)


def solution(mesh):
    in_specs = (
        P(("doc", "gram"), None),
        P(("gram", "doc"), None),
        P("doc", "gram", None, None, None),
        P("doc", "gram", None),
        P("doc", "gram", None),
        P("doc", "gram"),
    )
    out_specs = (P(("doc", "gram"), None), P(("gram", "doc"), None))
    return jax.shard_map(body, mesh=mesh, in_specs=in_specs, out_specs=out_specs, check_vma=False)
```

```python
import functools

import jax
import jax.numpy as jnp
from jax import lax
from jax.experimental import pallas as pl
from jax.experimental.pallas import tpu as pltpu
from jax.sharding import PartitionSpec as P

OUTER = 4
EXTRA = 8
STEP_RATIO = 6
STEP_SUM = 6
SCALE = 2.0**-5
FIRST_GROUP = (3,)
MIDDLE_GROUP = (0, 1)
LAST_GROUP = (2,)


def partner(outer, inner, by_outer, by_inner):
    return [
        ((o * inner + i), (o ^ by_outer) * inner + (i ^ by_inner))
        for o in range(outer)
        for i in range(inner)
    ]


def partial_sums(block):
    rows, k = block.shape
    return jnp.sum(block.astype(jnp.float32).reshape(rows // EXTRA, EXTRA, k), axis=0)


def visit_tiles(group, side, w_ref, counts, ready, acc, h_out, order, ratios, h_all, rows, cols, live):
    quarter = h_all.shape[0] // len(group)
    me_h = lax.axis_index("doc") // (lax.axis_size("doc") // OUTER)

    def quarter_of(slot):
        return (cols[0, 0, slot] * side) // quarter ^ me_h

    def scan(slot, found):
        near = quarter_of(slot)
        hit = near == group[0]
        for member in group[1:]:
            hit = hit | (near == member)
        order[found] = slot
        return found + jnp.where(hit, 1, 0)

    found = lax.fori_loop(0, live[0, 0], scan, 0)
    for extra in range(max(STEP_RATIO, STEP_SUM)):
        order[found + extra] = 0

    def tile_at(j):
        slot = order[j]
        near = quarter_of(slot)
        at = jnp.int32(0)
        for k, member in enumerate(group):
            at = jnp.where(near == member, k, at)
        row = pl.multiple_of(rows[0, 0, slot] * side, side)
        local = pl.multiple_of(lax.rem(cols[0, 0, slot] * side, quarter), side)
        return slot, row, at, local, pl.multiple_of(at * quarter + local, side)

    def make_ratios(step, carry):
        made = []
        for k in range(STEP_RATIO):
            j = step * STEP_RATIO + k
            slot, row, _, _, col = tile_at(j)
            model = lax.dot_general(
                w_ref[pl.ds(row, side), :],
                h_all[pl.ds(col, side), :],
                (((1,), (1,)), ((), ())),
                preferred_element_type=jnp.float32,
            )
            keep = jnp.where(j < found, 1.0, 0.0)
            made.append((counts[slot].astype(jnp.float32) / model * keep).astype(jnp.bfloat16))
        for k, ratio in enumerate(made):
            ratios[step * STEP_RATIO + k] = ratio
        return carry

    def add_terms(step, carry):
        terms = []
        for k in range(STEP_SUM):
            j = step * STEP_SUM + k
            slot, row, at, local, col = tile_at(j)
            ratio = ratios[j]
            w_part = jnp.dot(
                ratio, h_all[pl.ds(col, side), :], preferred_element_type=jnp.float32
            )
            h_part = lax.dot_general(
                ratio,
                w_ref[pl.ds(row, side), :],
                (((0,), (0,)), ((), ())),
                preferred_element_type=jnp.float32,
            )
            terms.append((row, at, local, w_part, h_part))
        for row, at, local, w_part, h_part in terms:
            acc[pl.ds(row, side), :] += w_part
            h_out[at, pl.ds(local, side), :] += h_part
        return carry

    if ready is not None:
        ready()
    lax.fori_loop(0, (found + STEP_RATIO - 1) // STEP_RATIO, make_ratios, 0)
    lax.fori_loop(0, (found + STEP_SUM - 1) // STEP_SUM, add_terms, 0)


def clear(h_out, quarter, w_sums):
    for at in range(h_out.shape[0]):
        h_out[at, :quarter, :] = jnp.zeros((quarter, h_out.shape[2]), jnp.float32)
        h_out[at, quarter:, :] = w_sums


def started(sems, first, *pairs):
    copies = [
        pltpu.make_async_copy(source, target, sems.at[first + k])
        for k, (source, target) in enumerate(pairs)
    ]
    for copy in copies:
        copy.start()
    return copies


def first_kernel(group, side, inner, rows_in, cols_in, live, stored, w_pieces, *refs):
    h_pieces, refs = refs[: len(group)], refs[len(group) :]
    w_block, acc, counts, w_sums, h_out, sems, order, ratios, h_all, rows, cols = refs
    places = started(sems, 0, (rows_in, rows), (cols_in, cols))
    (load,) = started(sems, 2, (stored.at[0, 0], counts))
    quarter = h_pieces[0].shape[0]
    w_len = w_block.shape[0]
    w_rows = w_len // (inner * OUTER)
    me_o = lax.axis_index("gram") // inner
    for o in range(OUTER):
        for i in range(inner):
            at = pl.multiple_of(((me_o ^ o) * inner + i) * w_rows, 16)
            w_block[pl.ds(at, w_rows), :] = w_pieces[i, o]
    for at, piece in enumerate(h_pieces):
        h_all[at * quarter : (at + 1) * quarter, :] = piece[...]
    acc[:w_len, :] = jnp.zeros((w_len, acc.shape[1]), jnp.float32)
    acc[w_len:, :] = partial_sums(h_all[...])
    w_sums[...] = partial_sums(w_block[...])
    clear(h_out, quarter, w_sums[...])
    for copy in places:
        copy.wait()
    visit_tiles(
        group, side, w_block, counts, load.wait, acc, h_out, order, ratios, h_all, rows, cols, live
    )


def middle_kernel(group, side, inner, rows_in, cols_in, live, counts, w_block, _, w_sums, *refs):
    mine, h_pieces, refs = refs[0], refs[1 : len(group)], refs[len(group) :]
    acc, h_out, sems, order, ratios, h_all, rows, cols = refs
    quarter = mine.shape[0]
    places = started(sems, 0, (rows_in, rows), (cols_in, cols))
    (load,) = started(sems, 2, (mine, h_all.at[pl.ds(0, quarter)]))
    w_len = w_block.shape[0]
    for at, piece in enumerate(h_pieces):
        h_all[(at + 1) * quarter : (at + 2) * quarter, :] = piece[...]
    clear(h_out, quarter, w_sums[...])
    for copy in places:
        copy.wait()
    visit_tiles(
        group, side, w_block, counts, load.wait, acc, h_out, order, ratios, h_all, rows, cols, live
    )
    acc[w_len:, :] += partial_sums(h_all[...])


def last_kernel(group, side, inner, rows_in, cols_in, live, counts, w_block, _, w_sums, *refs):
    h_pieces, refs = refs[: len(group)], refs[len(group) :]
    acc, h_out, w_outs, refs = refs[0], refs[1], refs[2 : 2 + inner], refs[2 + inner :]
    sems, order, ratios, h_all, rows, cols = refs
    quarter = h_pieces[0].shape[0]
    places = started(sems, 0, (rows_in, rows), (cols_in, cols))
    w_len = w_block.shape[0]
    w_rows = w_len // (inner * OUTER)
    for at, piece in enumerate(h_pieces):
        h_all[at * quarter : (at + 1) * quarter, :] = piece[...]
    acc[w_len:, :] += partial_sums(h_all[...])
    clear(h_out, quarter, w_sums[...])
    for copy in places:
        copy.wait()
    visit_tiles(
        group, side, w_block, counts, None, acc, h_out, order, ratios, h_all, rows, cols, live
    )
    me_w = lax.axis_index("gram")
    me_o, me_i = me_w // inner, lax.rem(me_w, inner)
    for i in range(inner):
        for o in range(OUTER):
            at = pl.multiple_of(((me_o ^ o) * inner + (me_i ^ i)) * w_rows, 8)
            w_outs[i][o, :w_rows, :] = acc[pl.ds(at, w_rows), :]
            w_outs[i][o, w_rows:, :] = acc[w_len:, :]


def finish_kernel(w_factor, h_factor, w_total, h_total, w_next, h_next):
    for factor, total, out in ((h_factor, h_total, h_next), (w_factor, w_total, w_next)):
        rows = factor.shape[0]
        denom = jnp.sum(total[rows:, :], axis=0, keepdims=True)
        out[...] = (factor[...].astype(jnp.float32) * total[:rows, :] / denom).astype(out.dtype)


def finish(w_factor, h_factor, w_total, h_total):
    vmem = pl.BlockSpec(memory_space=pltpu.VMEM)
    return pl.pallas_call(
        finish_kernel,
        out_shape=[jax.ShapeDtypeStruct(x.shape, x.dtype) for x in (w_factor, h_factor)],
        in_specs=[vmem] * 4,
        out_specs=[vmem] * 2,
        compiler_params=pltpu.CompilerParams(vmem_limit_bytes=16 * 1024 * 1024),
    )(w_factor, h_factor, w_total, h_total)


def in_hbm(x):
    return pltpu.with_memory_space_constraint(x, pltpu.HBM)


def run_kernel(kernel, group, inner, args, from_hbm, out_shapes, quarter, acc_shape):
    rows, cols, _, counts = args[:4]
    slots, side = counts.shape[-3:-1]
    topics = acc_shape[1]
    width = len(group)
    pad = max(STEP_RATIO, STEP_SUM)
    scratch = [
        pltpu.SemaphoreType.DMA((3,)),
        pltpu.SMEM((slots + pad,), jnp.int32),
        pltpu.VMEM((slots + pad, side, side), jnp.bfloat16),
        pltpu.VMEM((width * quarter, topics), jnp.bfloat16),
        pltpu.SMEM(rows.shape, rows.dtype),
        pltpu.SMEM(cols.shape, cols.dtype),
    ]
    spaces = [pltpu.HBM if at in from_hbm else pltpu.VMEM for at in range(len(args))]
    spaces[2] = pltpu.SMEM
    args = [in_hbm(x) if at in from_hbm else x for at, x in enumerate(args)]
    return pl.pallas_call(
        functools.partial(kernel, group, side, inner),
        out_shape=out_shapes,
        in_specs=[pl.BlockSpec(memory_space=space) for space in spaces],
        out_specs=[pl.BlockSpec(memory_space=pltpu.VMEM)] * len(out_shapes),
        scratch_shapes=scratch,
        input_output_aliases={} if kernel is first_kernel else {5: 0},
        compiler_params=pltpu.CompilerParams(vmem_limit_bytes=32 * 1024 * 1024),
        cost_estimate=pl.CostEstimate(
            flops=144 * width * side * side * topics, bytes_accessed=1 << 23, transcendentals=0
        ),
    )(*args)


def body(w_factor, h_factor, tile_counts, tile_rows, tile_cols, tile_live):
    doc, gram = lax.axis_size("doc"), lax.axis_size("gram")
    inner_h, inner_w = doc // OUTER, gram // OUTER
    w_rows, topics = w_factor.shape
    h_rows = h_factor.shape[0]
    w_len = w_rows * gram

    def send_h(x, by_outer, by_inner=0):
        return lax.ppermute(x, "doc", partner(OUTER, inner_h, by_outer, by_inner))

    def send_w(x, by_outer, by_inner=0):
        return lax.ppermute(x, "gram", partner(OUTER, inner_w, by_outer, by_inner))

    if inner_h > 1:
        ring = [[o * inner_h + i for i in range(inner_h)] for o in range(OUTER)]
        mine = lax.all_gather(h_factor, "doc", axis=0, tiled=True, axis_index_groups=ring)
    else:
        mine = h_factor
    quarter = mine.shape[0]
    h_pieces = {0: mine}
    w_got = [None] * 3
    w_got[1] = send_w(w_factor, 2)
    w_got[0] = send_w(w_factor, 1)
    w_got[2] = send_w(w_factor, 3)
    h_pieces[3] = send_h(mine, 3)
    later, w_got[0] = lax.optimization_barrier((mine, w_got[0]))
    h_pieces[1] = send_h(later, 1)
    h_pieces[2] = send_h(h_pieces[3], 1)
    w_outer = jnp.stack([w_factor] + w_got)
    pairs = [[o * inner_w + i for i in range(inner_w)] for o in range(OUTER)]
    w_pieces = lax.all_gather(w_outer, "gram", axis_index_groups=pairs)

    places = [tile_rows, tile_cols, tile_live]
    acc_shape = jax.ShapeDtypeStruct((w_len + EXTRA, topics), jnp.float32)
    h_shape = [
        jax.ShapeDtypeStruct((len(group), quarter + EXTRA, topics), jnp.float32)
        for group in (FIRST_GROUP, MIDDLE_GROUP, LAST_GROUP)
    ]
    sum_shape = jax.ShapeDtypeStruct((EXTRA, topics), jnp.float32)
    w_shape = jax.ShapeDtypeStruct((OUTER, w_rows + EXTRA, topics), jnp.float32)
    w_block, acc, counts, w_sums, far = run_kernel(
        first_kernel,
        FIRST_GROUP,
        inner_w,
        [*places, tile_counts, w_pieces, *[h_pieces[m] for m in FIRST_GROUP]],
        (0, 1, 3),
        [
            jax.ShapeDtypeStruct((w_len, topics), w_factor.dtype),
            acc_shape,
            jax.ShapeDtypeStruct(tile_counts.shape[2:], tile_counts.dtype),
            sum_shape,
            h_shape[0],
        ],
        quarter,
        acc_shape.shape,
    )
    h_scale = SCALE / 2
    far = send_h((far[0] * h_scale).astype(jnp.float16), 1)
    acc, middle = run_kernel(
        middle_kernel,
        MIDDLE_GROUP,
        inner_w,
        [*places, counts, w_block, acc, w_sums, *[h_pieces[m] for m in MIDDLE_GROUP]],
        (0, 1, 7),
        [acc_shape, h_shape[1]],
        quarter,
        acc_shape.shape,
    )
    _, last, *w_outs = run_kernel(
        last_kernel,
        LAST_GROUP,
        inner_w,
        [*places, counts, w_block, acc, w_sums, *[h_pieces[m] for m in LAST_GROUP]],
        (0, 1),
        [acc_shape, h_shape[2]] + [w_shape] * inner_w,
        quarter,
        acc_shape.shape,
    )
    terms = {0: middle[0], 1: middle[1], 2: last[0]}
    far, last, *w_outs = lax.optimization_barrier((far, last, *w_outs))
    terms[2] = last[0]
    across = (terms[2] * h_scale + far.astype(jnp.float32)).astype(jnp.float16)
    across = send_h(across, 2)

    w_scale = SCALE / inner_w
    w_got = [send_w(w_outs[i], 0, i) for i in range(1, inner_w)]
    w_terms = w_outs[0]
    for got in w_got:
        w_terms = w_terms + got
    near, w_terms = lax.optimization_barrier(((terms[1] * h_scale).astype(jnp.float16), w_terms))
    near = send_h(near, 1)
    w_sent = [
        send_w((w_terms[o] * w_scale).astype(jnp.float16), o) for o in range(OUTER - 1, 0, -1)
    ]

    h_total = terms[0] * h_scale + across.astype(jnp.float32) + near.astype(jnp.float32)
    if inner_h > 1:
        me_i = lax.rem(lax.axis_index("doc"), inner_h)
        tail = h_total[-EXTRA:]

        def share(i):
            part = lax.dynamic_slice_in_dim(h_total, (me_i ^ i) * h_rows, h_rows, 0)
            return jnp.concatenate([part, tail], axis=0)

        total = share(0)
        for i in range(1, inner_h):
            total = total + send_h(share(i), 0, i)
        h_total = total
    h_total, *w_sent = lax.optimization_barrier((h_total, *w_sent))
    w_total = w_terms[0] * w_scale
    for got in w_sent:
        w_total = w_total + got.astype(jnp.float32)
    w_next, h_next = finish(w_factor, h_factor, w_total, h_total)
    return (w_next, h_next)


def solution(mesh):
    in_specs = (
        P(("doc", "gram"), None),
        P(("gram", "doc"), None),
        P("doc", "gram", None, None, None),
        P("doc", "gram", None),
        P("doc", "gram", None),
        P("doc", "gram"),
    )
    out_specs = (P(("doc", "gram"), None), P(("gram", "doc"), None))
    return jax.shard_map(body, mesh=mesh, in_specs=in_specs, out_specs=out_specs, check_vma=False)
```

```python
import functools

import jax
import jax.numpy as jnp
from jax import lax
from jax.experimental import pallas as pl
from jax.experimental.pallas import tpu as pltpu
from jax.sharding import PartitionSpec as P

OUTER = 4
EXTRA = 8
STEP_RATIO = 8
STEP_SUM = 4
SCALE = 2.0**-5
FIRST_GROUP = (3,)
MIDDLE_GROUP = (0, 1)
LAST_GROUP = (2,)


def partner(outer, inner, by_outer, by_inner):
    return [
        ((o * inner + i), (o ^ by_outer) * inner + (i ^ by_inner))
        for o in range(outer)
        for i in range(inner)
    ]


def partial_sums(block):
    rows, k = block.shape
    return jnp.sum(block.astype(jnp.float32).reshape(rows // EXTRA, EXTRA, k), axis=0)


def visit_tiles(group, side, w_ref, counts, ready, acc, h_out, order, ratios, h_all, rows, cols, live):
    quarter = h_all.shape[0] // len(group)
    me_h = lax.axis_index("doc") // (lax.axis_size("doc") // OUTER)

    def quarter_of(slot):
        return (cols[0, 0, slot] * side) // quarter ^ me_h

    def scan(slot, found):
        near = quarter_of(slot)
        hit = near == group[0]
        for member in group[1:]:
            hit = hit | (near == member)
        order[found] = slot
        return found + jnp.where(hit, 1, 0)

    found = lax.fori_loop(0, live[0, 0], scan, 0)
    for extra in range(max(STEP_RATIO, STEP_SUM)):
        order[found + extra] = 0

    def tile_at(j):
        slot = order[j]
        near = quarter_of(slot)
        at = jnp.int32(0)
        for k, member in enumerate(group):
            at = jnp.where(near == member, k, at)
        row = pl.multiple_of(rows[0, 0, slot] * side, side)
        local = pl.multiple_of(lax.rem(cols[0, 0, slot] * side, quarter), side)
        return slot, row, at, local, pl.multiple_of(at * quarter + local, side)

    def make_ratios(step, carry):
        made = []
        for k in range(STEP_RATIO):
            j = step * STEP_RATIO + k
            slot, row, _, _, col = tile_at(j)
            model = lax.dot_general(
                w_ref[pl.ds(row, side), :],
                h_all[pl.ds(col, side), :],
                (((1,), (1,)), ((), ())),
                preferred_element_type=jnp.float32,
            )
            keep = jnp.where(j < found, 1.0, 0.0)
            made.append((counts[slot].astype(jnp.float32) / model * keep).astype(jnp.bfloat16))
        for k, ratio in enumerate(made):
            ratios[step * STEP_RATIO + k] = ratio
        return carry

    def add_terms(step, carry):
        terms = []
        for k in range(STEP_SUM):
            j = step * STEP_SUM + k
            slot, row, at, local, col = tile_at(j)
            ratio = ratios[j]
            w_part = jnp.dot(
                ratio, h_all[pl.ds(col, side), :], preferred_element_type=jnp.float32
            )
            h_part = lax.dot_general(
                ratio,
                w_ref[pl.ds(row, side), :],
                (((0,), (0,)), ((), ())),
                preferred_element_type=jnp.float32,
            )
            terms.append((row, at, local, w_part, h_part))
        for row, at, local, w_part, h_part in terms:
            acc[pl.ds(row, side), :] += w_part
            h_out[at, pl.ds(local, side), :] += h_part
        return carry

    if ready is not None:
        ready()
    lax.fori_loop(0, (found + STEP_RATIO - 1) // STEP_RATIO, make_ratios, 0)
    lax.fori_loop(0, (found + STEP_SUM - 1) // STEP_SUM, add_terms, 0)


def clear(h_out, quarter, w_sums):
    for at in range(h_out.shape[0]):
        h_out[at, :quarter, :] = jnp.zeros((quarter, h_out.shape[2]), jnp.float32)
        h_out[at, quarter:, :] = w_sums


def started(sems, first, *pairs):
    copies = [
        pltpu.make_async_copy(source, target, sems.at[first + k])
        for k, (source, target) in enumerate(pairs)
    ]
    for copy in copies:
        copy.start()
    return copies


def first_kernel(group, side, inner, rows_in, cols_in, live, stored, w_pieces, *refs):
    h_pieces, refs = refs[: len(group)], refs[len(group) :]
    w_block, acc, counts, w_sums, h_out, sems, order, ratios, h_all, rows, cols = refs
    places = started(sems, 0, (rows_in, rows), (cols_in, cols))
    (load,) = started(sems, 2, (stored.at[0, 0], counts))
    quarter = h_pieces[0].shape[0]
    w_len = w_block.shape[0]
    w_rows = w_len // (inner * OUTER)
    me_o = lax.axis_index("gram") // inner
    for o in range(OUTER):
        for i in range(inner):
            at = pl.multiple_of(((me_o ^ o) * inner + i) * w_rows, 16)
            w_block[pl.ds(at, w_rows), :] = w_pieces[i, o]
    for at, piece in enumerate(h_pieces):
        h_all[at * quarter : (at + 1) * quarter, :] = piece[...]
    acc[:w_len, :] = jnp.zeros((w_len, acc.shape[1]), jnp.float32)
    acc[w_len:, :] = partial_sums(h_all[...])
    w_sums[...] = partial_sums(w_block[...])
    clear(h_out, quarter, w_sums[...])
    for copy in places:
        copy.wait()
    visit_tiles(
        group, side, w_block, counts, load.wait, acc, h_out, order, ratios, h_all, rows, cols, live
    )


def middle_kernel(group, side, inner, rows_in, cols_in, live, counts, w_block, _, w_sums, *refs):
    mine, h_pieces, refs = refs[0], refs[1 : len(group)], refs[len(group) :]
    acc, h_out, sems, order, ratios, h_all, rows, cols = refs
    quarter = mine.shape[0]
    places = started(sems, 0, (rows_in, rows), (cols_in, cols))
    (load,) = started(sems, 2, (mine, h_all.at[pl.ds(0, quarter)]))
    w_len = w_block.shape[0]
    for at, piece in enumerate(h_pieces):
        h_all[(at + 1) * quarter : (at + 2) * quarter, :] = piece[...]
    clear(h_out, quarter, w_sums[...])
    for copy in places:
        copy.wait()
    visit_tiles(
        group, side, w_block, counts, load.wait, acc, h_out, order, ratios, h_all, rows, cols, live
    )
    acc[w_len:, :] += partial_sums(h_all[...])


def last_kernel(group, side, inner, rows_in, cols_in, live, counts, w_block, _, w_sums, *refs):
    h_pieces, refs = refs[: len(group)], refs[len(group) :]
    acc, h_out, w_outs, refs = refs[0], refs[1], refs[2 : 2 + inner], refs[2 + inner :]
    sems, order, ratios, h_all, rows, cols = refs
    quarter = h_pieces[0].shape[0]
    places = started(sems, 0, (rows_in, rows), (cols_in, cols))
    w_len = w_block.shape[0]
    w_rows = w_len // (inner * OUTER)
    for at, piece in enumerate(h_pieces):
        h_all[at * quarter : (at + 1) * quarter, :] = piece[...]
    acc[w_len:, :] += partial_sums(h_all[...])
    clear(h_out, quarter, w_sums[...])
    for copy in places:
        copy.wait()
    visit_tiles(
        group, side, w_block, counts, None, acc, h_out, order, ratios, h_all, rows, cols, live
    )
    me_w = lax.axis_index("gram")
    me_o, me_i = me_w // inner, lax.rem(me_w, inner)
    for i in range(inner):
        for o in range(OUTER):
            at = pl.multiple_of(((me_o ^ o) * inner + (me_i ^ i)) * w_rows, 8)
            w_outs[i][o, :w_rows, :] = acc[pl.ds(at, w_rows), :]
            w_outs[i][o, w_rows:, :] = acc[w_len:, :]


def finish_kernel(w_factor, h_factor, w_total, h_total, w_next, h_next, w_out, h_out, sems):
    copies = []
    for factor, total, out, target in (
        (h_factor, h_total, h_out, h_next),
        (w_factor, w_total, w_out, w_next),
    ):
        rows = factor.shape[0]
        denom = jnp.sum(total[rows:, :], axis=0, keepdims=True)
        out[...] = (factor[...].astype(jnp.float32) * total[:rows, :] / denom).astype(out.dtype)
        copies.append(pltpu.make_async_copy(out, target, sems.at[len(copies)]))
        copies[-1].start()
    for copy in copies:
        copy.wait()


def finish(w_factor, h_factor, w_total, h_total):
    vmem = pl.BlockSpec(memory_space=pltpu.VMEM)
    factors = (w_factor, h_factor)
    return pl.pallas_call(
        finish_kernel,
        out_shape=[jax.ShapeDtypeStruct(x.shape, x.dtype) for x in factors],
        in_specs=[vmem] * 4,
        out_specs=[pl.BlockSpec(memory_space=pl.ANY)] * 2,
        scratch_shapes=[
            *[pltpu.VMEM(x.shape, x.dtype) for x in factors],
            pltpu.SemaphoreType.DMA((2,)),
        ],
        compiler_params=pltpu.CompilerParams(vmem_limit_bytes=16 * 1024 * 1024),
    )(w_factor, h_factor, w_total, h_total)


def in_hbm(x):
    return pltpu.with_memory_space_constraint(x, pltpu.HBM)


def run_kernel(kernel, group, inner, args, from_hbm, out_shapes, quarter, acc_shape):
    rows, cols, _, counts = args[:4]
    slots, side = counts.shape[-3:-1]
    topics = acc_shape[1]
    width = len(group)
    pad = max(STEP_RATIO, STEP_SUM)
    scratch = [
        pltpu.SemaphoreType.DMA((3,)),
        pltpu.SMEM((slots + pad,), jnp.int32),
        pltpu.VMEM((slots + pad, side, side), jnp.bfloat16),
        pltpu.VMEM((width * quarter, topics), jnp.bfloat16),
        pltpu.SMEM(rows.shape, rows.dtype),
        pltpu.SMEM(cols.shape, cols.dtype),
    ]
    spaces = [pltpu.HBM if at in from_hbm else pltpu.VMEM for at in range(len(args))]
    spaces[2] = pltpu.SMEM
    args = [in_hbm(x) if at in from_hbm else x for at, x in enumerate(args)]
    return pl.pallas_call(
        functools.partial(kernel, group, side, inner),
        out_shape=out_shapes,
        in_specs=[pl.BlockSpec(memory_space=space) for space in spaces],
        out_specs=[pl.BlockSpec(memory_space=pltpu.VMEM)] * len(out_shapes),
        scratch_shapes=scratch,
        input_output_aliases={} if kernel is first_kernel else {5: 0},
        compiler_params=pltpu.CompilerParams(vmem_limit_bytes=32 * 1024 * 1024),
        cost_estimate=pl.CostEstimate(
            flops=36 * width * side * side * topics, bytes_accessed=1 << 23, transcendentals=0
        ),
    )(*args)


def body(w_factor, h_factor, tile_counts, tile_rows, tile_cols, tile_live):
    doc, gram = lax.axis_size("doc"), lax.axis_size("gram")
    inner_h, inner_w = doc // OUTER, gram // OUTER
    w_rows, topics = w_factor.shape
    h_rows = h_factor.shape[0]
    w_len = w_rows * gram

    def send_h(x, by_outer, by_inner=0):
        return lax.ppermute(x, "doc", partner(OUTER, inner_h, by_outer, by_inner))

    def send_w(x, by_outer, by_inner=0):
        return lax.ppermute(x, "gram", partner(OUTER, inner_w, by_outer, by_inner))

    if inner_h > 1:
        ring = [[o * inner_h + i for i in range(inner_h)] for o in range(OUTER)]
        mine = lax.all_gather(h_factor, "doc", axis=0, tiled=True, axis_index_groups=ring)
    else:
        mine = h_factor
    quarter = mine.shape[0]
    h_pieces = {0: mine}
    h_pieces[3] = send_h(mine, 3)
    w_got = [send_w(w_factor, o) for o in range(1, OUTER)]
    h_pieces[2] = send_h(h_pieces[3], 1)
    later, w_got[0] = lax.optimization_barrier((mine, w_got[0]))
    h_pieces[1] = send_h(later, 1)
    w_outer = jnp.stack([w_factor] + w_got)
    pairs = [[o * inner_w + i for i in range(inner_w)] for o in range(OUTER)]
    w_pieces = lax.all_gather(w_outer, "gram", axis_index_groups=pairs)

    places = [tile_rows, tile_cols, tile_live]
    acc_shape = jax.ShapeDtypeStruct((w_len + EXTRA, topics), jnp.float32)
    h_shape = [
        jax.ShapeDtypeStruct((len(group), quarter + EXTRA, topics), jnp.float32)
        for group in (FIRST_GROUP, MIDDLE_GROUP, LAST_GROUP)
    ]
    sum_shape = jax.ShapeDtypeStruct((EXTRA, topics), jnp.float32)
    w_shape = jax.ShapeDtypeStruct((OUTER, w_rows + EXTRA, topics), jnp.float32)
    w_block, acc, counts, w_sums, far = run_kernel(
        first_kernel,
        FIRST_GROUP,
        inner_w,
        [*places, tile_counts, w_pieces, *[h_pieces[m] for m in FIRST_GROUP]],
        (0, 1, 3),
        [
            jax.ShapeDtypeStruct((w_len, topics), w_factor.dtype),
            acc_shape,
            jax.ShapeDtypeStruct(tile_counts.shape[2:], tile_counts.dtype),
            sum_shape,
            h_shape[0],
        ],
        quarter,
        acc_shape.shape,
    )
    h_scale = SCALE / 2
    far = send_h((far[0] * h_scale).astype(jnp.float16), 1)
    acc, middle = run_kernel(
        middle_kernel,
        MIDDLE_GROUP,
        inner_w,
        [*places, counts, w_block, acc, w_sums, *[h_pieces[m] for m in MIDDLE_GROUP]],
        (0, 1, 7),
        [acc_shape, h_shape[1]],
        quarter,
        acc_shape.shape,
    )
    _, last, *w_outs = run_kernel(
        last_kernel,
        LAST_GROUP,
        inner_w,
        [*places, counts, w_block, acc, w_sums, *[h_pieces[m] for m in LAST_GROUP]],
        (0, 1),
        [acc_shape, h_shape[2]] + [w_shape] * inner_w,
        quarter,
        acc_shape.shape,
    )
    terms = {0: middle[0], 1: middle[1], 2: last[0]}
    far, *w_outs = lax.optimization_barrier((far, *w_outs))
    across = (terms[2] * h_scale + far.astype(jnp.float32)).astype(jnp.float16)
    across = send_h(across, 2)

    w_scale = SCALE / inner_w
    w_got = [send_w(w_outs[i], 0, i) for i in range(1, inner_w)]
    near = (terms[1][:quarter] * h_scale).astype(jnp.float16)
    near, *w_got = lax.optimization_barrier((near, *w_got))
    near = send_h(near, 1)
    w_terms = w_outs[0]
    for got in w_got:
        w_terms = w_terms + got
    w_sent = [
        send_w((w_terms[o] * w_scale).astype(jnp.float16), o) for o in range(1, OUTER)
    ]

    near = jnp.concatenate([near, far[quarter:]])
    h_total = terms[0] * h_scale + across.astype(jnp.float32) + near.astype(jnp.float32)
    if inner_h > 1:
        me_i = lax.rem(lax.axis_index("doc"), inner_h)
        tail = h_total[-EXTRA:]

        def share(i):
            part = lax.dynamic_slice_in_dim(h_total, (me_i ^ i) * h_rows, h_rows, 0)
            return jnp.concatenate([part, tail], axis=0)

        total = share(0)
        for i in range(1, inner_h):
            total = total + send_h(share(i), 0, i)
        h_total = total
    h_total, *w_sent = lax.optimization_barrier((h_total, *w_sent))
    w_total = w_terms[0] * w_scale
    for got in w_sent:
        w_total = w_total + got.astype(jnp.float32)
    w_next, h_next = finish(w_factor, h_factor, w_total, h_total)
    return (w_next, h_next)


def solution(mesh):
    in_specs = (
        P(("doc", "gram"), None),
        P(("gram", "doc"), None),
        P("doc", "gram", None, None, None),
        P("doc", "gram", None),
        P("doc", "gram", None),
        P("doc", "gram"),
    )
    out_specs = (P(("doc", "gram"), None), P(("gram", "doc"), None))
    return jax.shard_map(body, mesh=mesh, in_specs=in_specs, out_specs=out_specs, check_vma=False)
```
